32 devices in a mesh: groups: 2 (over x), wide: 8 (over z, y), narrow: 2 (over core).
Axes of the slice: x: 2, y: 2, z: 4, core: 2. Of those that a mesh axis runs over, the one named last changes fastest.
Arguments:
- density: bfloat16 [128, 2, 256, 384], P(('groups', 'wide'), None, 'narrow'), parts along dimension 0, may hold values from -6 to 6
- block_order: int32 [128], P('groups'), parts along dimension 0, may hold values from 0 to 63, as said below
- pattern: int32 [6, 128], P(None, 'groups'), parts along dimension 1, may hold values 0 or 1
- factors: bfloat16 [6, 128, 2, 2, 256, 256], P(None, ('groups', 'wide'), None, None, 'narrow'), parts along dimension 1, may hold values from -0.1875 to 0.1875
- near: bfloat16 [128, 3, 2, 256, 256], P(('groups', 'wide'), None, None, 'narrow'), parts along dimension 0, may hold values from -0.15625 to 0.15625
Outputs:
- potential: float32 [128, 2, 256, 384], P(('groups', 'wide'), None, 'narrow'), parts along dimension 0
The draws below stay inside these ranges and needn't reach their ends.
There are 2 independent parts, one for each index of `groups`. The reference program is written for one: setup_inputs(seed, part) draws one part's arguments, and reference() takes and returns one part's arrays. A program takes and returns all parts, laid end to end along the dimension named above; each array names one. Nothing has to cross between parts.
Inputs may be any that keep to these rules, and one draw needn't show every extreme that they name: `block_order`: a permutation of the blocks; position d * 8 + j (j < 8) holds block (d xor m_j) * 8 + s_j, where the masks m_j (0 .. 7) and the slot permutation s_j depend only on j.
All inputs are finite; a program needn't handle non-finite values.
Results may differ from the reference program's by a relative error of at most 0.0044.
Values may be sent and summed in bfloat16 or wider, within the bound.
A program may use at most 128 MiB of HBM per device.

```python
import jax
import jax.numpy as jnp

BLOCK = 256
LEVELS = 6
RHS = 384
BLOCKS = 64
BLK_DEV = 8


def draw_block_order(key, part):
    key = jax.random.fold_in(key, 11)
    mask_key = jax.random.fold_in(key, 1)
    slot_key = jax.random.fold_in(key, 2)
    device_count = BLOCKS // BLK_DEV
    masks = jax.random.randint(mask_key, (BLK_DEV,), 0, device_count, dtype=jnp.int32)
    slots = jax.random.permutation(slot_key, BLK_DEV).astype(jnp.int32)
    devices = jnp.arange(device_count, dtype=jnp.int32)[:, None]
    source = jnp.bitwise_xor(devices, masks[None, :]) * BLK_DEV + slots[None, :]
    return source.reshape((BLOCKS,)).astype(jnp.int32)


def plant(drawn, own_key, least, largest):
    longest = drawn.shape.index(max(drawn.shape))
    spots = []
    for shift in (0, 1):
        where = [jax.random.randint(jax.random.fold_in(own_key, axis), (), 0, length) for axis, length in enumerate(drawn.shape)]
        where[longest] = (where[longest] + shift) % drawn.shape[longest]
        spots.append(tuple(where))
    return drawn.at[spots[0]].set(least).at[spots[1]].set(largest)


def shard_levels(rng, dims, split, least, largest):
    loudness = 1.0
    for position, parts in split:
        draws = jax.random.uniform(jax.random.fold_in(jax.random.fold_in(rng, 6), position), (parts,), jnp.float32, least / len(split), largest / len(split))
        loudness = loudness * jnp.repeat(jnp.exp(draws), dims[position] // parts).reshape((-1,) + (1,) * (len(dims) - 1 - position))
    return loudness


def centred(key, extent, width, bound, split=(), kind=jnp.bfloat16):
    factor_of = shard_levels(key, extent, split, -0.22, 0.18) if split else 1.0
    array = jax.random.normal(key, extent, jnp.float32) * width * factor_of
    return jnp.minimum(jnp.maximum(array, -bound), bound).astype(kind)


def setup_inputs(seed: int = 0, part: int = 0) -> dict:
    seeds = jax.random.split(jax.random.key(seed), 6)
    part_splits = jax.random.split(jax.random.fold_in(seeds[5], part), 6)
    return {
        "density": centred(part_splits[0], (BLOCKS, 2, BLOCK, RHS), 1.0, 6.0, ((0, 8), (2, 2))),
        "block_order": draw_block_order(jax.random.fold_in(jax.random.fold_in(seeds[5], part), 71), part),
        "pattern": plant((jax.random.randint(part_splits[2], (LEVELS, BLOCKS), 0, 4) < 3).astype(jnp.int32), jax.random.fold_in(part_splits[2], 1), 0, 1),
        "factors": centred(part_splits[3], (LEVELS, BLOCKS, 2, 2, BLOCK, BLOCK), (4 * BLOCK) ** -0.5, 0.1875, ((1, 8), (4, 2))),
        "near": centred(part_splits[4], (BLOCKS, 3, 2, BLOCK, BLOCK), (6 * BLOCK) ** -0.5, 0.15625, ((0, 8), (3, 2))),
    }


def complex_apply(matrix, vector):
    mat_re = matrix[:, 0].astype(jnp.float32)
    mat_im = matrix[:, 1].astype(jnp.float32)
    vec_re = vector[:, 0].astype(jnp.float32)
    vec_im = vector[:, 1].astype(jnp.float32)
    real_part = jnp.einsum('boi,bir->bor', mat_re, vec_re) - jnp.einsum('boi,bir->bor', mat_im, vec_im)
    imag_part = jnp.einsum('boi,bir->bor', mat_im, vec_re) + jnp.einsum('boi,bir->bor', mat_re, vec_im)
    return jnp.stack([real_part, imag_part], 1)


def pair_local(vector, bit_pos):
    total = vector.shape[0]
    stride = 1 << bit_pos
    folded = vector.reshape((total // (2 * stride), 2, stride) + vector.shape[1:])
    return folded[:, ::-1].reshape(vector.shape)


def reference(density, block_order, pattern, factors, near):
    initial = jnp.take(density, block_order.astype(jnp.int32), axis=0)
    current = initial
    summed = None
    for level_idx in range(LEVELS):
        partner = pair_local(current, level_idx)
        keep = pattern[level_idx].astype(jnp.float32)[:, None, None, None]
        summed = complex_apply(factors[level_idx, :, 0], current) + keep * complex_apply(factors[level_idx, :, 1], partner)
        if level_idx < LEVELS - 1:
            current = summed.astype(jnp.bfloat16)
    zero_block = jnp.zeros_like(initial[:1])
    left_block = jnp.concatenate([zero_block, initial[:-1]], 0)
    right_block = jnp.concatenate([initial[1:], zero_block], 0)
    nearby = complex_apply(near[:, 0], left_block) + complex_apply(near[:, 1], initial) + complex_apply(near[:, 2], right_block)
    return summed + nearby
```

```python
import functools

import jax
import jax.numpy as jnp
from jax import lax
from jax.experimental import pallas as pl
from jax.experimental.pallas import tpu as pltpu
from jax.sharding import PartitionSpec as P

LEVELS = 6
LANES = 128
MESH = pl.DeviceIdType.MESH


def flipped(index, distance):
    return index + distance * (1 - 2 * lax.rem(lax.div(index, distance), 2))


def kernel(
    n_wide, x_ref, bits_ref, keep_ref, factors_hbm, near_hbm, out_ref,
    fac, nea, rbuf, xs, full, part, halo, load_sem, send_sem, recv_sem,
):
    chunks, count, rows, lanes = x_ref.shape
    bits = n_wide.bit_length() - 1
    local_bits = count.bit_length() - 1
    me = lax.axis_index("wide")
    core = lax.axis_index("narrow")
    own = pl.ds(pl.multiple_of(core * rows, rows), rows)

    loads = [
        pltpu.make_async_copy(factors_hbm.at[l], fac.at[l], load_sem.at[l]) for l in range(LEVELS)
    ] + [pltpu.make_async_copy(near_hbm, nea, load_sem.at[LEVELS])]
    for load in loads:
        load.start()

    barrier = pltpu.get_barrier_semaphore()
    for other in range(1, n_wide):
        pl.semaphore_signal(
            barrier, inc=1, device_id={"wide": lax.rem(me + other, n_wide)}, device_id_type=MESH
        )
    pl.semaphore_signal(barrier, inc=1, device_id={"narrow": 1 - core}, device_id_type=MESH)
    pl.semaphore_wait(barrier, n_wide)

    made = []
    loaded = set()

    def remote(src, dst, device):
        index = len(made)
        copy = pltpu.make_async_remote_copy(
            src_ref=src, dst_ref=dst, send_sem=send_sem.at[index], recv_sem=recv_sem.at[index],
            device_id=device, device_id_type=MESH,
        )
        made.append(copy)
        return copy

    sibling = {"narrow": 1 - core}
    order = list(range(bits))[::-1]
    route, narrow, wide, forward, rightward, leftward = {}, {}, {}, {}, {}, {}
    for c in range(chunks):
        for i, k in enumerate(order):
            src = x_ref.at[c] if i == 0 else xs.at[i - 1, c]
            route[c, i] = remote(src, rbuf.at[i, c], {"wide": flipped(me, 1 << k)})
        for l in range(LEVELS):
            half = full.at[l, c, :, own, :]
            narrow[c, l] = remote(half, half, sibling)
            if l >= local_bits:
                w = l - local_bits
                held = part.at[w, c, :, own, :]
                wide[c, l] = remote(half, held, {"wide": flipped(me, 1 << w)})
                forward[c, l] = remote(held, held, sibling)
    for c in range(chunks):
        rightward[c] = remote(
            full.at[0, c, count - 1], halo.at[c, 0], {"wide": lax.rem(me + 1, n_wide)}
        )
        leftward[c] = remote(
            full.at[0, c, 0], halo.at[c, 1], {"wide": lax.rem(me + n_wide - 1, n_wide)}
        )

    def need(index):
        if index not in loaded:
            loaded.add(index)
            loads[index].wait()

    def joined(product):
        real = product[:rows, :LANES] - product[rows:, LANES:]
        imag = product[rows:, :LANES] + product[:rows, LANES:]
        return real, imag

    def dot(left, right):
        return jnp.dot(left, right, preferred_element_type=jnp.float32)

    def begin(c):
        if c > 0:
            route[c - 1, 0].wait_send()
        route[c, 0].start()

    def pick(c, i):
        route[c, i].wait_recv()
        last = i == bits - 1

        @pl.loop(0, count)
        def _(j):
            held = x_ref[c, j] if i == 0 else xs[i - 1, c, j]
            value = jnp.where(bits_ref[i, j] != 0, rbuf[i, c, j], held)
            if last:
                full[0, c, j, own, :] = value
            else:
                xs[i, c, j] = value

        if last:
            narrow[c, 0].start()
            if local_bits == 0:
                wide[c, 0].start()
        else:
            route[c, i + 1].start()

    def pass_on(c, l):
        wide[c, l].wait_recv()
        forward[c, l].start()

    def level(c, l):
        need(l)
        narrow[c, l].wait_recv()
        if l == 0:
            @pl.when(me < n_wide - 1)
            def _():
                rightward[c].start()

            @pl.when(me > 0)
            def _():
                leftward[c].start()

        if l >= local_bits:
            forward[c, l].wait_recv()

        @pl.loop(0, count)
        def _(b):
            mine = dot(fac[l, b, 0], full[l, c, b])
            if l < local_bits:
                other = full[l, c, flipped(b, 1 << l)]
            else:
                other = part[l - local_bits, c, b]
            product = mine + keep_ref[l, b] * dot(fac[l, b, 1], other)
            real, imag = joined(product)
            if l < LEVELS - 1:
                full[l + 1, c, b, own, :LANES] = real.astype(jnp.bfloat16)
                full[l + 1, c, b, own, LANES:] = imag.astype(jnp.bfloat16)
            else:
                at = slice(c * LANES, (c + 1) * LANES)
                out_ref[b, 0, :, at] = out_ref[b, 0, :, at] + real
                out_ref[b, 1, :, at] = out_ref[b, 1, :, at] + imag

        if l < LEVELS - 1:
            if l + 1 >= local_bits:
                wide[c, l + 1].start()
            narrow[c, l + 1].start()

    def nearby(c):
        need(LEVELS)
        at = slice(c * LANES, (c + 1) * LANES)

        @pl.when(me > 0)
        def _():
            rightward[c].wait_recv()

        @pl.when(me == 0)
        def _():
            halo[c, 0] = jnp.zeros_like(halo[c, 0])

        @pl.when(me < n_wide - 1)
        def _():
            leftward[c].wait_recv()

        @pl.when(me == n_wide - 1)
        def _():
            halo[c, 1] = jnp.zeros_like(halo[c, 1])

        def put(b, left, right):
            product = dot(nea[b, 0], left) + dot(nea[b, 1], full[0, c, b]) + dot(nea[b, 2], right)
            real, imag = joined(product)
            out_ref[b, 0, :, at] = real
            out_ref[b, 1, :, at] = imag

        put(0, halo[c, 0], full[0, c, 1])

        @pl.loop(1, count - 1)
        def _(b):
            put(b, full[0, c, b - 1], full[0, c, b + 1])

        put(count - 1, full[0, c, count - 2], halo[c, 1])

    hop = 10.0
    steps = []
    for c in range(chunks):
        now = 2 * hop * c
        steps.append((now, functools.partial(begin, c)))
        for i, k in enumerate(order):
            now += 2 * hop if i == 0 else hop
            steps.append((now, functools.partial(pick, c, i)))
        for l in range(LEVELS):
            now += 2.0
            if l >= local_bits:
                now += hop if l < LEVELS - 1 else 2 * hop
                steps.append((now, functools.partial(pass_on, c, l)))
                now += 2.0
            steps.append((now, functools.partial(level, c, l)))
            if l == local_bits:
                steps.append((now + 0.5, functools.partial(nearby, c)))
    for _, step in sorted(steps, key=lambda item: item[0]):
        step()

    for c in range(chunks):
        for i in range(bits):
            if not (i == 0 and c < chunks - 1):
                route[c, i].wait_send()
        for l in range(LEVELS):
            narrow[c, l].wait_send()
            if l >= local_bits:
                wide[c, l].wait_send()
                forward[c, l].wait_send()

    @pl.when(me < n_wide - 1)
    def _():
        for c in range(chunks):
            rightward[c].wait_send()

    @pl.when(me > 0)
    def _():
        for c in range(chunks):
            leftward[c].wait_send()


def per_device(density, block_order, pattern, factors, near):
    count, _, rows, columns = density.shape
    n_wide = lax.axis_size("wide")
    bits = n_wide.bit_length() - 1
    chunks = columns // LANES
    exchanged = LEVELS - (count.bit_length() - 1)
    wide_at = lax.axis_index("wide")
    wanted = lax.dynamic_slice_in_dim(block_order, wide_at * count, count)
    masks = (wanted // count) ^ wide_at
    taken = jnp.take(density, wanted % count, axis=0)
    x = taken.reshape(count, 2, rows, chunks, LANES).transpose(3, 0, 2, 1, 4)
    x = x.reshape(chunks, count, rows, 2 * LANES)
    swap = jnp.stack([(masks >> k) & 1 for k in range(bits)[::-1]]).astype(jnp.int32)
    keep = lax.dynamic_slice_in_dim(pattern, wide_at * count, count, 1).astype(jnp.float32)
    size = factors.shape[-1]
    factors = factors.reshape(LEVELS, count, 2, 2 * rows, size)
    near = near.reshape(count, 3, 2 * rows, size)
    copies = chunks * (bits + LEVELS + 2 * exchanged + 2)
    bf16 = jnp.bfloat16
    return pl.pallas_call(
        functools.partial(kernel, n_wide),
        out_shape=jax.ShapeDtypeStruct((count, 2, rows, columns), jnp.float32),
        in_specs=[
            pl.BlockSpec(memory_space=pltpu.VMEM),
            pl.BlockSpec(memory_space=pltpu.SMEM),
            pl.BlockSpec(memory_space=pltpu.SMEM),
            pl.BlockSpec(memory_space=pl.ANY),
            pl.BlockSpec(memory_space=pl.ANY),
        ],
        out_specs=pl.BlockSpec(memory_space=pltpu.VMEM),
        scratch_shapes=[
            pltpu.VMEM(factors.shape, bf16),
            pltpu.VMEM(near.shape, bf16),
            pltpu.VMEM((bits,) + x.shape, bf16),
            pltpu.VMEM((max(bits - 1, 1),) + x.shape, bf16),
            pltpu.VMEM((LEVELS, chunks, count, size, 2 * LANES), bf16),
            pltpu.VMEM((exchanged, chunks, count, size, 2 * LANES), bf16),
            pltpu.VMEM((chunks, 2, size, 2 * LANES), bf16),
            pltpu.SemaphoreType.DMA((LEVELS + 1,)),
            pltpu.SemaphoreType.DMA((copies,)),
            pltpu.SemaphoreType.DMA((copies,)),
        ],
        compiler_params=pltpu.CompilerParams(
            collective_id=0, has_side_effects=True, vmem_limit_bytes=62 * 1024 * 1024
        ),
        cost_estimate=pl.CostEstimate(
            flops=2 * 4 * count * (2 * LEVELS + 3) * rows * size * columns,
            bytes_accessed=2 * (factors.size + near.size + x.size) + 4 * x.size,
            transcendentals=0,
        ),
    )(x, swap, keep, factors, near)


def solution(mesh):
    return jax.shard_map(
        per_device,
        mesh=mesh,
        in_specs=(
            P(("groups", "wide"), None, "narrow", None),
            P("groups"),
            P(None, "groups"),
            P(None, ("groups", "wide"), None, None, "narrow", None),
            P(("groups", "wide"), None, None, "narrow", None),
        ),
        out_specs=P(("groups", "wide"), None, "narrow", None),
        check_vma=False,
    )
```

```python
import functools

import jax
import jax.numpy as jnp
from jax import lax
from jax.experimental import pallas as pl
from jax.experimental.pallas import tpu as pltpu
from jax.sharding import PartitionSpec as P

LEVELS = 6
LANES = 128
GROUPS = 2
SERIAL = False
MESH = pl.DeviceIdType.MESH


def flipped(index, distance):
    return index + distance * (1 - 2 * lax.rem(lax.div(index, distance), 2))


def flipped_bits(index, other):
    return index ^ other


def kernel(
    n_wide, density_ref, order_ref, pattern_ref, factors_hbm, near_hbm, out_ref,
    fac, nea, rbuf, xs, full, part, halo, load_sem, send_sem, recv_sem,
):
    chunks, count, rows, lanes = xs.shape[1:]
    pieces = [pl.ds(g * (count // GROUPS), count // GROUPS) for g in range(GROUPS)]
    spans = [(g * (count // GROUPS), (g + 1) * (count // GROUPS)) for g in range(GROUPS)]
    bits = n_wide.bit_length() - 1
    local_bits = count.bit_length() - 1
    me = lax.axis_index("wide")
    core = lax.axis_index("narrow")
    own = pl.ds(pl.multiple_of(core * rows, rows), rows)

    loads = [
        pltpu.make_async_copy(factors_hbm.at[l], fac.at[l], load_sem.at[l]) for l in range(LEVELS)
    ] + [pltpu.make_async_copy(near_hbm, nea, load_sem.at[LEVELS])]
    for load in loads:
        load.start()

    barrier = pltpu.get_barrier_semaphore()
    for other in range(1, n_wide):
        pl.semaphore_signal(
            barrier, inc=1, device_id={"wide": lax.rem(me + other, n_wide)}, device_id_type=MESH
        )
    pl.semaphore_signal(barrier, inc=1, device_id={"narrow": 1 - core}, device_id_type=MESH)

    def take(c):
        at = slice(c * LANES, (c + 1) * LANES)

        @pl.loop(0, count)
        def _(j):
            slot = lax.rem(order_ref[me * count + j], count)
            xs[0, c, j, :, :LANES] = density_ref[slot, 0, :, at]
            xs[0, c, j, :, LANES:] = density_ref[slot, 1, :, at]

    for c in range(chunks):
        take(c)
    pl.semaphore_wait(barrier, n_wide)

    made = []
    loaded = set()

    def remote(src, dst, device):
        index = len(made)
        copy = pltpu.make_async_remote_copy(
            src_ref=src, dst_ref=dst, send_sem=send_sem.at[index], recv_sem=recv_sem.at[index],
            device_id=device, device_id_type=MESH,
        )
        made.append(copy)
        return copy

    sibling = {"narrow": 1 - core}
    order = list(range(bits))[::-1]
    route, narrow, wide, forward, rightward, leftward = {}, {}, {}, {}, {}, {}
    for c in range(chunks):
        for i, k in enumerate(order):
            for g, piece in enumerate(pieces):
                route[c, g, i] = remote(
                    xs.at[i, c, piece], rbuf.at[i, c, piece], {"wide": flipped(me, 1 << k)}
                )
        for l in range(LEVELS):
            for g, piece in enumerate(pieces):
                half = full.at[l, c, piece, own, :]
                narrow[c, g, l] = remote(half, half, sibling)
                if l >= local_bits:
                    w = l - local_bits
                    held = part.at[w, c, piece, own, :]
                    wide[c, g, l] = remote(half, held, {"wide": flipped(me, 1 << w)})
                    forward[c, g, l] = remote(held, held, sibling)
    for c in range(chunks):
        rightward[c] = remote(
            full.at[0, c, count - 1], halo.at[c, 0], {"wide": lax.rem(me + 1, n_wide)}
        )
        leftward[c] = remote(
            full.at[0, c, 0], halo.at[c, 1], {"wide": lax.rem(me + n_wide - 1, n_wide)}
        )

    def need(index):
        if index not in loaded:
            loaded.add(index)
            loads[index].wait()

    def joined(product):
        real = product[:rows, :LANES] - product[rows:, LANES:]
        imag = product[rows:, :LANES] + product[:rows, LANES:]
        return real, imag

    def dot(left, right):
        return jnp.dot(left, right, preferred_element_type=jnp.float32)

    sent = set()

    def begin(c, g):
        before = (c, g - 1, 0) if g else (c - 1, GROUPS - 1, 0)
        if SERIAL and c + g > 0:
            route[before].wait_send()
            sent.add(before)
        route[c, g, 0].start()

    def pick(c, g, i):
        route[c, g, i].wait_recv()
        last = i == bits - 1

        @pl.loop(*spans[g])
        def _(j):
            mask = flipped_bits(lax.div(order_ref[me * count + j], count), me)
            bit = lax.rem(lax.div(mask, 1 << order[i]), 2)
            value = jnp.where(bit != 0, rbuf[i, c, j], xs[i, c, j])
            if last:
                full[0, c, j, own, :] = value
            else:
                xs[i + 1, c, j] = value

        if last:
            narrow[c, g, 0].start()
        else:
            route[c, g, i + 1].start()

    def pass_on(c, g, l):
        wide[c, g, l].wait_recv()
        forward[c, g, l].start()

    def edges(c):
        for g in range(GROUPS):
            narrow[c, g, 0].wait_recv()

        @pl.when(me < n_wide - 1)
        def _():
            rightward[c].start()

        @pl.when(me > 0)
        def _():
            leftward[c].start()

    def apply(c, g, l):
        @pl.loop(*spans[g])
        def _(b):
            mine = dot(fac[l, b, 0], full[l, c, b])
            if l < local_bits:
                other = full[l, c, flipped(b, 1 << l)]
            else:
                other = part[l - local_bits, c, b]
            keep = pattern_ref[l, me * count + b].astype(jnp.float32)
            product = mine + keep * dot(fac[l, b, 1], other)
            real, imag = joined(product)
            if l < LEVELS - 1:
                full[l + 1, c, b, own, :LANES] = real.astype(jnp.bfloat16)
                full[l + 1, c, b, own, LANES:] = imag.astype(jnp.bfloat16)
            else:
                at = slice(c * LANES, (c + 1) * LANES)
                out_ref[b, 0, :, at] = out_ref[b, 0, :, at] + real
                out_ref[b, 1, :, at] = out_ref[b, 1, :, at] + imag

        if l < LEVELS - 1:
            if l + 1 >= local_bits:
                wide[c, g, l + 1].start()
            narrow[c, g, l + 1].start()

    def level_local(c, l):
        need(l)
        if l == 0:
            edges(c)
        else:
            for g in range(GROUPS):
                narrow[c, g, l].wait_recv()
        for g in range(GROUPS):
            apply(c, g, l)

    def level_wide(c, g, l):
        need(l)
        narrow[c, g, l].wait_recv()
        forward[c, g, l].wait_recv()
        apply(c, g, l)

    def nearby(c):
        need(LEVELS)
        at = slice(c * LANES, (c + 1) * LANES)

        @pl.when(me > 0)
        def _():
            rightward[c].wait_recv()

        @pl.when(me == 0)
        def _():
            halo[c, 0] = jnp.zeros_like(halo[c, 0])

        @pl.when(me < n_wide - 1)
        def _():
            leftward[c].wait_recv()

        @pl.when(me == n_wide - 1)
        def _():
            halo[c, 1] = jnp.zeros_like(halo[c, 1])

        def put(b, left, right):
            product = dot(nea[b, 0], left) + dot(nea[b, 1], full[0, c, b]) + dot(nea[b, 2], right)
            real, imag = joined(product)
            out_ref[b, 0, :, at] = real
            out_ref[b, 1, :, at] = imag

        put(0, halo[c, 0], full[0, c, 1])

        @pl.loop(1, count - 1)
        def _(b):
            put(b, full[0, c, b - 1], full[0, c, b + 1])

        put(count - 1, full[0, c, count - 2], halo[c, 1])

    hop = 9.0 / GROUPS
    free = {}

    def travel(bit, ready):
        start = max(ready, free.get(bit, 0.0))
        free[bit] = start + hop * (2.0 if bit == bits - 1 else 1.0)
        return start, free[bit]

    steps = []
    ready = {}
    for c in range(chunks):
        for g in range(GROUPS):
            now = 0.0
            for i, k in enumerate(order):
                start, now = travel(k, now)
                if i == 0:
                    steps.append((start, functools.partial(begin, c, g)))
                steps.append((now, functools.partial(pick, c, g, i)))
            ready[c, g] = now
    for c in range(chunks):
        now = max(ready[c, g] for g in range(GROUPS))
        for l in range(local_bits):
            now += 2.0
            steps.append((now, functools.partial(level_local, c, l)))
        steps.append((now + 0.5, functools.partial(nearby, c)))
        for g in range(GROUPS):
            then = now
            for l in range(local_bits, LEVELS):
                _, then = travel(l - local_bits, then)
                steps.append((then, functools.partial(pass_on, c, g, l)))
                then += 2.0
                steps.append((then, functools.partial(level_wide, c, g, l)))
    for _, step in sorted(steps, key=lambda item: item[0]):
        step()

    for key, copy in route.items():
        if key not in sent:
            copy.wait_send()
    for copies in (narrow, wide, forward):
        for copy in copies.values():
            copy.wait_send()

    @pl.when(me < n_wide - 1)
    def _():
        for c in range(chunks):
            rightward[c].wait_send()

    @pl.when(me > 0)
    def _():
        for c in range(chunks):
            leftward[c].wait_send()


def per_device(density, block_order, pattern, factors, near):
    count, _, rows, columns = density.shape
    n_wide = lax.axis_size("wide")
    bits = n_wide.bit_length() - 1
    chunks = columns // LANES
    exchanged = LEVELS - (count.bit_length() - 1)
    shape = (chunks, count, rows, 2 * LANES)
    size = factors.shape[-1]
    factors = factors.reshape(LEVELS, count, 2, 2 * rows, size)
    near = near.reshape(count, 3, 2 * rows, size)
    copies = chunks * (GROUPS * (bits + LEVELS + 2 * exchanged) + 2)
    bf16 = jnp.bfloat16
    return pl.pallas_call(
        functools.partial(kernel, n_wide),
        out_shape=jax.ShapeDtypeStruct((count, 2, rows, columns), jnp.float32),
        in_specs=[
            pl.BlockSpec(memory_space=pltpu.VMEM),
            pl.BlockSpec(memory_space=pltpu.SMEM),
            pl.BlockSpec(memory_space=pltpu.SMEM),
            pl.BlockSpec(memory_space=pl.ANY),
            pl.BlockSpec(memory_space=pl.ANY),
        ],
        out_specs=pl.BlockSpec(memory_space=pltpu.VMEM),
        scratch_shapes=[
            pltpu.VMEM(factors.shape, bf16),
            pltpu.VMEM(near.shape, bf16),
            pltpu.VMEM((bits,) + shape, bf16),
            pltpu.VMEM((bits,) + shape, bf16),
            pltpu.VMEM((LEVELS, chunks, count, size, 2 * LANES), bf16),
            pltpu.VMEM((exchanged, chunks, count, size, 2 * LANES), bf16),
            pltpu.VMEM((chunks, 2, size, 2 * LANES), bf16),
            pltpu.SemaphoreType.DMA((LEVELS + 1,)),
            pltpu.SemaphoreType.DMA((copies,)),
            pltpu.SemaphoreType.DMA((copies,)),
        ],
        compiler_params=pltpu.CompilerParams(
            collective_id=0, has_side_effects=True, vmem_limit_bytes=62 * 1024 * 1024
        ),
        cost_estimate=pl.CostEstimate(
            flops=2 * 4 * count * (2 * LEVELS + 3) * rows * size * columns,
            bytes_accessed=2 * (factors.size + near.size + density.size) + 4 * density.size,
            transcendentals=0,
        ),
    )(density, block_order, pattern, factors, near)


def solution(mesh):
    return jax.shard_map(
        per_device,
        mesh=mesh,
        in_specs=(
            P(("groups", "wide"), None, "narrow", None),
            P("groups"),
            P(None, "groups"),
            P(None, ("groups", "wide"), None, None, "narrow", None),
            P(("groups", "wide"), None, None, "narrow", None),
        ),
        out_specs=P(("groups", "wide"), None, "narrow", None),
        check_vma=False,
    )
```
